512 devices in a mesh: leaf: 256 (over z, x, y), vec: 2 (over core).
Axes of the slice: x: 4, y: 4, z: 16, core: 2. Of those that a mesh axis runs over, the one named last changes fastest.
Arguments:
- vectors: float32 [256, 524288], P('vec', 'leaf'), may hold values from -6 to 6
- points: bfloat16 [3, 524288], P(None, 'leaf'), may hold values from 0 to 1
- basis: bfloat16 [524288, 128], P('leaf'), may hold values from -0.25 to 0.25
- near_list: int32 [1024, 7], P('leaf'), may hold values from -1 to 1023, as said below
- transfer_leaf: bfloat16 [131072, 128], P('leaf'), may hold values from -0.5 to 0.5
- transfer_one: bfloat16 [65536, 128], P('leaf'), may hold values from -0.5 to 0.5
- transfer_two: bfloat16 [32768, 128], P('leaf'), may hold values from -0.5 to 0.5
- transfer_three: bfloat16 [16384, 128], P('leaf'), may hold values from -0.5 to 0.5
- couple_zero: bfloat16 [4096, 128, 128], P('leaf'), as said below
- couple_one: bfloat16 [2048, 128, 128], P('leaf'), as said below
- couple_two: bfloat16 [1024, 128, 128], P('leaf'), as said below
- couple_three: bfloat16 [512, 128, 128], P('leaf'), as said below
- couple_four: bfloat16 [256, 128, 128], P('leaf'), as said below
Outputs:
- products: float32 [256, 524288], P('vec', 'leaf')
The draws below stay inside these ranges and needn't reach their ends.
Inputs may be any that keep to these rules, and one draw needn't show every extreme that they name: `near_list`: row l holds leaf l and, in any order and without repeats, some of the leaves l - 3 to l + 3 other than l; every other entry is -1. A row l that is a multiple of 4 holds every leaf from l - 3 to l + 3 that lies in 0 to 1023. `couple_zero`: A block 4 t + j whose cluster t + o_j lies outside the level is zero. `couple_one`: Likewise. `couple_two`: Likewise. `couple_three`: Likewise. `couple_four`: Likewise.
All inputs are finite; a program needn't handle non-finite values.
Results may differ from the reference program's by a relative error of at most 0.013.
Values may be sent and summed in bfloat16 or wider, within the bound.
A program may use at most 64 MiB of HBM per device.

```python
import jax
import jax.numpy as jnp
from jax import lax

P_SIZE = 512
R = 128
NV = 256
LEAVES_DEV = 4
NEARM = 7
NLEAF = 1024
NPTS = 524288


def draw_near_list(key, part):
    leaf_ids = jnp.arange(NLEAF, dtype=jnp.int32)
    moves = jnp.array([-3, -2, -1, 1, 2, 3], jnp.int32)
    keep_bits = jax.random.randint(jax.random.fold_in(key, 3), (NLEAF, 6), 0, 2)
    keep_bits = jnp.where((leaf_ids % LEAVES_DEV == 0)[:, None], 1, keep_bits)
    candidate = leaf_ids[:, None] + moves[None, :]
    usable = (keep_bits == 1) & (candidate >= 0) & (candidate < NLEAF)
    others = jnp.where(usable, candidate, -1)
    rows_all = jnp.concatenate([leaf_ids[:, None], others], axis=1)
    row_keys = jax.random.split(jax.random.fold_in(key, 5), NLEAF)
    orders = jax.vmap(lambda row_key: jax.random.permutation(row_key, NEARM))(row_keys)
    return jnp.take_along_axis(rows_all, orders, axis=1).astype(jnp.int32)


def coupling_draw(key, level):
    cluster_count = NLEAF // 2 ** level
    block_ids = jnp.arange(cluster_count * 4, dtype=jnp.int32)
    cluster = block_ids // 4
    moves = jnp.array([-3, -2, 2, 3], jnp.int32)[block_ids % 4]
    source = cluster + moves
    usable = (source >= 0) & (source < cluster_count)
    local_key = jax.random.fold_in(key, 11 + level)
    values = jax.random.normal(local_key, (cluster_count * 4, R, R), jnp.float32)
    values = values * R ** (-0.5) * usable.astype(jnp.float32)[:, None, None]
    return values.astype(jnp.bfloat16)


def draw_couple_zero(key, part):
    return coupling_draw(key, 0)


def draw_couple_one(key, part):
    return coupling_draw(key, 1)


def draw_couple_two(key, part):
    return coupling_draw(key, 2)


def draw_couple_three(key, part):
    return coupling_draw(key, 3)


def draw_couple_four(key, part):
    return coupling_draw(key, 4)


def shard_levels(key, extent, shards, least, top_value):
    level, own = 1.0, jax.random.fold_in(key, 6)
    for position, parts in shards:
        steps = jnp.exp(jax.random.uniform(jax.random.fold_in(own, position), (parts,), jnp.float32, least / len(shards), top_value / len(shards)))
        level = level * jnp.repeat(steps, extent[position] // parts).reshape([-1 if axis == position else 1 for axis in range(len(extent))])
    return level


def centred(stream_key, shape, deviation, most, shards=(), held_as=jnp.bfloat16):
    gain = shard_levels(stream_key, shape, shards, -0.22, 0.18) if shards else 1.0
    result = jax.random.normal(stream_key, shape, jnp.float32) * deviation * gain
    return jnp.minimum(jnp.maximum(result, -most), most).astype(held_as)


def setup_inputs(seed: int = 0) -> dict:
    key_list = jax.random.split(jax.random.key(seed), 14)
    return {
        "vectors": centred(key_list[0], (NV, NPTS), 1.0, 6.0, ((0, 2), (1, 256)), jnp.float32),
        "points": jnp.clip(1.0 * jax.random.uniform(key_list[1], (3, NPTS), jnp.float32) ** shard_levels(key_list[1], (3, NPTS), ((1, 256),), -0.2, 0.2), 0.0, 1.0).astype(jnp.bfloat16),
        "basis": centred(key_list[2], (NPTS, R), P_SIZE ** -0.5, 0.25, ((0, 256),)),
        "near_list": draw_near_list(jax.random.fold_in(key_list[13], 71), 0),
        "transfer_leaf": centred(key_list[4], (NLEAF * R, R), R ** -0.5, 0.5, ((0, 256),)),
        "transfer_one": centred(key_list[5], (NLEAF // 2 * R, R), R ** -0.5, 0.5, ((0, 256),)),
        "transfer_two": centred(key_list[6], (NLEAF // 4 * R, R), R ** -0.5, 0.5, ((0, 256),)),
        "transfer_three": centred(key_list[7], (NLEAF // 8 * R, R), R ** -0.5, 0.5, ((0, 256),)),
        "couple_zero": draw_couple_zero(jax.random.fold_in(key_list[13], 71), 0),
        "couple_one": draw_couple_one(jax.random.fold_in(key_list[13], 71), 0),
        "couple_two": draw_couple_two(jax.random.fold_in(key_list[13], 71), 0),
        "couple_three": draw_couple_three(jax.random.fold_in(key_list[13], 71), 0),
        "couple_four": draw_couple_four(jax.random.fold_in(key_list[13], 71), 0),
    }


sharpness = 40.0
offsets = (-3, -2, 2, 3)


def kernel_blocks(target, sources, live_mask):
    distance = (target[0][None, :, None] - sources[0][:, None, :]) ** 2
    distance = distance + (target[1][None, :, None] - sources[1][:, None, :]) ** 2
    distance = distance + (target[2][None, :, None] - sources[2][:, None, :]) ** 2
    return (jnp.exp(-sharpness * distance) * live_mask[:, None, None]).astype(jnp.bfloat16)


def climb(low_level, transfer):
    matrices = transfer.reshape(-1, R, R).astype(jnp.float32)
    summands = jnp.einsum('lrs,lrv->lsv', matrices, low_level.astype(jnp.float32))
    return summands[0::2] + summands[1::2]


def couple(low_level, blocks):
    cluster_count = low_level.shape[0]
    matrices = blocks.reshape(cluster_count, 4, R, R).astype(jnp.float32)
    padded = jnp.pad(low_level.astype(jnp.float32), ((3, 3), (0, 0), (0, 0)))
    total = jnp.zeros((cluster_count, R, NV), jnp.float32)
    for slot_pos, move_by in enumerate(offsets):
        sources = padded[3 + move_by:3 + move_by + cluster_count]
        total = total + jnp.einsum('trs,tsv->trv', matrices[:, slot_pos], sources)
    return total


def reference(vectors, points, basis, near_list, transfer_leaf, transfer_one, transfer_two, transfer_three, couple_zero, couple_one, couple_two, couple_three, couple_four):
    vec_low = vectors.astype(jnp.bfloat16)
    point_grid = points.astype(jnp.float32).reshape(3, NLEAF, P_SIZE)
    vec_grid = vec_low.reshape(NV, NLEAF, P_SIZE)

    def near_leaf(leaf_pos):
        listed = near_list[leaf_pos]
        live_mask = (listed >= 0).astype(jnp.float32)
        source_ids = jnp.clip(listed, 0, NLEAF - 1).astype(jnp.int32)
        target = point_grid[:, leaf_pos, :]
        sources = jnp.take(point_grid, source_ids, axis=1)
        tiles = kernel_blocks(target, sources, live_mask)
        source_vecs = jnp.take(vec_grid, source_ids, axis=1)
        return jnp.einsum('vmq,mpq->vp', source_vecs.astype(jnp.float32), tiles.astype(jnp.float32))

    near_parts = lax.map(near_leaf, jnp.arange(NLEAF, dtype=jnp.int32))
    near_field = jnp.transpose(near_parts, (1, 0, 2)).reshape(NV, NPTS)

    basis_grid = basis.reshape(NLEAF, P_SIZE, R).astype(jnp.float32)
    leaf_coef = jnp.einsum('lpr,vlp->lrv', basis_grid, vec_grid.astype(jnp.float32))
    lows = [leaf_coef.astype(jnp.bfloat16)]
    transfers = (transfer_leaf, transfer_one, transfer_two, transfer_three)
    for transfer in transfers:
        lows.append(climb(lows[-1], transfer).astype(jnp.bfloat16))
    blocks_all = (couple_zero, couple_one, couple_two, couple_three, couple_four)
    fars = [couple(lows[level], blocks_all[level]) for level in range(5)]
    down_level = fars[4]
    for level in (3, 2, 1, 0):
        down_low = down_level.astype(jnp.bfloat16)
        matrices = transfers[level].reshape(-1, R, R).astype(jnp.float32)
        parents = jnp.repeat(down_low, 2, axis=0).astype(jnp.float32)
        down_level = fars[level] + jnp.einsum('lrs,lsv->lrv', matrices, parents)
    down_low = down_level.astype(jnp.bfloat16).astype(jnp.float32)
    far_field = jnp.einsum('lpr,lrv->vlp', basis_grid, down_low).reshape(NV, NPTS)
    return near_field + far_field
```

```python
import functools
import math

import jax
import jax.numpy as jnp
from jax import lax
from jax.experimental import pallas as pl
from jax.experimental.pallas import tpu as pltpu
from jax.sharding import PartitionSpec as P

MESH = pl.DeviceIdType.MESH
bf16 = jnp.bfloat16
f32 = jnp.float32
SCALE = 80.0 * math.log2(math.e)
NT = (((1,), (1,)), ((), ()))


def nn(a, b):
    return jnp.dot(a, b, preferred_element_type=f32)


def nt(a, b):
    return lax.dot_general(a, b, NT, preferred_element_type=f32)


def split3(value):
    high = value.astype(bf16).astype(f32)
    rest = value - high
    middle = rest.astype(bf16).astype(f32)
    low = (rest - middle).astype(bf16).astype(f32)
    return high, middle, low


def stack_rows(rows, count):
    width = rows[0].shape[1]
    place = lax.broadcasted_iota(jnp.int32, (count, width), 0)
    out = jnp.zeros((count, width), f32)
    for r, row in enumerate(rows):
        out = jnp.where(place == r, jnp.broadcast_to(row, (count, width)), out)
    return out


class Links:
    def __init__(self, send_sem, recv_sem, core):
        self.send_sem, self.recv_sem, self.core = send_sem, recv_sem, core
        self.count = 0
        self.sent = []

    def new(self, src, dst, target, can_send, can_recv):
        slot = self.count
        self.count += 1
        copy = pltpu.make_async_remote_copy(
            src_ref=src,
            dst_ref=dst,
            send_sem=self.send_sem.at[slot],
            recv_sem=self.recv_sem.at[slot],
            device_id=(target, self.core),
            device_id_type=MESH,
        )
        self.sent.append((copy, can_send))
        return copy, can_send, can_recv

    @staticmethod
    def start(message):
        copy, can_send, _ = message
        if can_send is True:
            copy.start()
        else:
            pl.when(can_send)(copy.start)

    @staticmethod
    def arrive(message):
        copy, _, can_recv = message
        if can_recv is True:
            copy.wait_recv()
        else:
            pl.when(can_recv)(copy.wait_recv)

    def drain(self):
        for copy, can_send in self.sent:
            if can_send is True:
                copy.wait_send()
            else:
                pl.when(can_send)(copy.wait_send)


def kernel(
    size,
    vec_hbm, pts_hbm, basis_hbm, near_ref, e0_hbm, e1_hbm, e2_hbm, e3_hbm,
    c0_hbm, c1_hbm, c2_hbm, c3_hbm, c4_hbm,
    out_hbm,
    vec_in, pts, basis, e0, e1, e2, e3, c0, c1, c2, c3, c4,
    vw, gw, fw, l0, l1, l2own, l2, p3s, p3r, p4s, p4r, l3s, l3r, l4s, l4r,
    f3s, f3r, f4s, f4r, far0, near,
    load_sem, send_sem, recv_sem, out_sem,
):
    i = lax.axis_index("leaf")
    core = lax.axis_index("vec")
    half = i % 2
    y = i % 4
    pair = i + 1 - 2 * half
    line = (pair, i + 2 - 4 * ((i // 2) % 2), i + 3 - 2 * y)
    step4 = 4 * (y - 3 + 3 * (y // 2))

    def inside(d):
        return (d >= 0) & (d < size)

    three_to = (i + 6 - 10 * half, i + 4 - 10 * half)
    three_from = (i - 6 + 10 * half, i - 4 + 10 * half)
    barrier = pltpu.get_barrier_semaphore()

    def greet(target):
        pl.semaphore_signal(barrier, inc=1, device_id=(target, core), device_id_type=MESH)

    wanted = jnp.int32(0)
    for move in (-3, -2, -1, 1, 2, 3):
        pl.when(inside(i + move))(functools.partial(greet, i + move))
        wanted = wanted + inside(i + move).astype(jnp.int32)
    for source, target in zip(
        (*three_from, i + step4), (*three_to, i - step4), strict=True
    ):
        pl.when(inside(source))(functools.partial(greet, source))
        wanted = wanted + inside(target).astype(jnp.int32)

    loads = []

    def load(src, dst):
        copy = pltpu.make_async_copy(src, dst, load_sem.at[len(loads)])
        copy.start()
        loads.append(copy)
        return copy

    load_pts = load(pts_hbm, pts)
    load_vec = [
        load(vec_hbm.at[:, pl.ds(512 * l, 512)], vec_in.at[l]) for l in range(4)
    ]
    load_basis = [
        load(basis_hbm.at[pl.ds(512 * l, 512)], basis.at[l]) for l in range(4)
    ]
    load_e0 = load(e0_hbm, e0)
    load_e1 = load(e1_hbm, e1)
    load_e2 = load(e2_hbm, e2)
    load_e3 = load(e3_hbm, e3.at[pl.ds(pl.multiple_of(64 * half, 64), 64)])
    load_c = [
        load(s, d)
        for s, d in ((c4_hbm, c4), (c3_hbm, c3), (c2_hbm, c2), (c1_hbm, c1), (c0_hbm, c0))
    ]

    gw[:, 16:, :] = jnp.zeros((10, 112, 512), bf16)
    load_pts.wait()
    for l in range(4):
        x = pts[:, 512 * l : 512 * (l + 1)].astype(f32)
        rows = [x[k : k + 1] for k in range(3)]
        scaled = split3(x * SCALE)
        square = rows[0] * rows[0] + rows[1] * rows[1] + rows[2] * rows[2]
        squares = list(split3(square * (-0.5 * SCALE)))
        one = jnp.ones_like(square)
        cols = [s[k : k + 1] for s in scaled for k in range(3)]
        gw[3 + l, 0:16, :] = stack_rows(cols + [one] * 3 + squares, 16).astype(bf16)
        target_rows = stack_rows(rows * 3 + squares + [one] * 3, 16)
        padded = jnp.concatenate([target_rows, jnp.zeros((112, 512), f32)], axis=0)
        fw[l] = jnp.transpose(padded).astype(bf16)

    for l in range(4):
        load_vec[l].wait()
        vw[3 + l] = vec_in[l].astype(bf16)
    for l in range(4):
        load_basis[l].wait()
        l0[3 + l] = nn(vw[3 + l], basis[l]).astype(bf16)
    load_e0.wait()
    for t in range(2):
        l1[3 + t] = (nn(l0[3 + 2 * t], e0[2 * t]) + nn(l0[4 + 2 * t], e0[2 * t + 1])).astype(bf16)
    load_e1.wait()
    l2own[...] = (nn(l1[3], e1[0]) + nn(l1[4], e1[1])).astype(bf16)
    load_e2.wait()
    share3 = nn(l2own[...], e2[...])
    p3s[...] = share3.astype(bf16)

    def clear(ref):
        ref[...] = jnp.zeros(ref.shape, ref.dtype)

    def clear_all(*refs):
        for ref in refs:
            clear(ref)

    pl.when(i < 1)(lambda: clear_all(vw.at[0:3], gw.at[0:3, 0:16], l0.at[0:3], l1.at[1:3]))
    pl.when(i < 2)(lambda: clear_all(l1.at[0:1], l2.at[1]))
    pl.when(i < 3)(lambda: clear_all(l2.at[0]))
    pl.when(i > size - 2)(lambda: clear_all(vw.at[7:10], gw.at[7:10, 0:16], l0.at[7:10], l1.at[5:7]))
    pl.when(i > size - 3)(lambda: clear_all(l1.at[7:8], l2.at[2]))
    pl.when(i > size - 4)(lambda: clear_all(l2.at[3]))
    for k in range(2):
        pl.when(jnp.logical_not(inside(three_from[k])))(functools.partial(clear, l3r.at[k]))
    pl.when(jnp.logical_not(inside(i + step4)))(functools.partial(clear, l4r))

    links = Links(send_sem, recv_sem, core)

    def shift(src, dst, move):
        return links.new(src, dst, i + move, inside(i + move), inside(i - move))

    e3_rows = e3.at[pl.ds(pl.multiple_of(64 * half, 64), 64)]
    m_e3 = links.new(e3_rows, e3_rows, pair, True, True)
    m_p3 = links.new(p3s, p3r, pair, True, True)
    m_vec = []
    m_pts = []
    for k in range(3):
        m_vec.append(
            (shift(vw.at[6 - k], vw.at[2 - k], 1), shift(vw.at[3 + k], vw.at[7 + k], -1))
        )
        m_pts.append(
            (
                shift(gw.at[6 - k, pl.ds(0, 16)], gw.at[2 - k, pl.ds(0, 16)], 1),
                shift(gw.at[3 + k, pl.ds(0, 16)], gw.at[7 + k, pl.ds(0, 16)], -1),
            )
        )
    m_l0 = (
        shift(l0.at[pl.ds(4, 3)], l0.at[pl.ds(0, 3)], 1),
        shift(l0.at[pl.ds(3, 3)], l0.at[pl.ds(7, 3)], -1),
    )
    m_l1 = (
        shift(l1.at[pl.ds(3, 2)], l1.at[pl.ds(1, 2)], 1),
        shift(l1.at[pl.ds(3, 2)], l1.at[pl.ds(5, 2)], -1),
        shift(l1.at[4], l1.at[0], 2),
        shift(l1.at[3], l1.at[7], -2),
    )
    m_l2 = (
        shift(l2own, l2.at[0], 3),
        shift(l2own, l2.at[1], 2),
        shift(l2own, l2.at[2], -2),
        shift(l2own, l2.at[3], -3),
    )
    m_p4 = [links.new(p4s, p4r.at[k], line[k], True, True) for k in range(3)]
    m_l3 = [
        links.new(l3s, l3r.at[k], three_to[k], inside(three_to[k]), inside(three_from[k]))
        for k in range(2)
    ]
    m_l4 = links.new(l4s, l4r, i - step4, inside(i - step4), inside(i + step4))
    m_f3 = links.new(f3s, f3r, pair, True, True)
    m_f4 = [links.new(f4s, f4r.at[k], line[k], True, True) for k in range(3)]

    load_e3.wait()
    pl.semaphore_wait(barrier, wanted)

    for m in (m_e3, m_p3, *m_pts[0], *m_vec[0], *m_l2, *m_l1):
        links.start(m)
    for m in (*m_pts[1], *m_vec[1], *m_pts[2], *m_vec[2], *m_l0):
        links.start(m)

    def live(l, w):
        leaf = i * 4 + w - 3
        found = jnp.float32(0.0)
        for m in range(7):
            found = jnp.where(near_ref[l, m] == leaf, jnp.float32(1.0), found)
        return jnp.where(leaf >= 0, found, jnp.float32(0.0))

    def tile(l, w):
        block = jnp.exp2(nn(fw[l], gw[w])).astype(bf16)
        picked = vw[w] * live(l, w).astype(bf16)
        return nt(picked, block)

    def own_leaf(l, carry):
        total = tile(l, 3)
        for w in range(4, 7):
            total = total + tile(l, w)
        near[l] = total
        return carry

    lax.fori_loop(0, 1, own_leaf, 0)

    links.arrive(m_e3)
    links.arrive(m_p3)
    l3s[...] = (share3 + p3r[...].astype(f32)).astype(bf16)
    share4 = nn(p3s[...], e3[...])
    p4s[...] = share4.astype(bf16)
    for m in (*m_p4, *m_l3):
        links.start(m)

    lax.fori_loop(1, 2, own_leaf, 0)

    total4 = share4
    for k in range(3):
        links.arrive(m_p4[k])
        total4 = total4 + p4r[k].astype(f32)
    l4s[...] = total4.astype(bf16)
    links.start(m_l4)

    lax.fori_loop(2, 3, own_leaf, 0)

    for copy in load_c:
        copy.wait()
    for m in m_l3:
        links.arrive(m)
    far3 = nt(l3r[0], c3[0]) + nt(l3r[1], c3[1])
    f3s[...] = far3.astype(bf16)
    links.start(m_f3)
    links.arrive(m_l4)
    far4 = nt(l4r[...], c4[0])
    f4s[...] = far4.astype(bf16)
    for m in m_f4:
        links.start(m)

    lax.fori_loop(3, 4, own_leaf, 0)

    for m in (*m_pts[0], *m_vec[0]):
        links.arrive(m)

    def beside(l, carry):
        near[l] = near[l] + tile(l, 2)
        near[l + 1] = near[l + 1] + tile(l + 1, 7)
        return carry

    lax.fori_loop(0, 3, beside, 0)

    for m in (*m_l1, *m_l2):
        links.arrive(m)
    links.arrive(m_f3)
    for m in m_f4:
        links.arrive(m)
    down4 = far4
    for k in range(3):
        down4 = down4 + f4r[k].astype(f32)
    down3 = far3 + f3r[...].astype(f32) + nt(down4.astype(bf16), e3[...])
    far2 = nt(l2[0], c2[0]) + nt(l2[1], c2[1]) + nt(l2[2], c2[2]) + nt(l2[3], c2[3])
    down2 = (far2 + nt(down3.astype(bf16), e2[...])).astype(bf16)
    down1 = []
    for t in range(2):
        far1 = nt(l1[t], c1[4 * t]) + nt(l1[1 + t], c1[4 * t + 1])
        far1 = far1 + nt(l1[5 + t], c1[4 * t + 2]) + nt(l1[6 + t], c1[4 * t + 3])
        down1.append((far1 + nt(down2, e1[t])).astype(bf16))
    for l in range(4):
        far0[l] = nt(down1[l // 2], e0[l])

    for m in (*m_pts[1], *m_vec[1]):
        links.arrive(m)

    def second(l, carry):
        near[l] = near[l] + tile(l, 1)
        near[l + 2] = near[l + 2] + tile(l + 2, 8)
        return carry

    lax.fori_loop(0, 2, second, 0)

    for m in (*m_pts[2], *m_vec[2]):
        links.arrive(m)
    near[0] = near[0] + tile(0, 0)
    near[3] = near[3] + tile(3, 9)

    for m in m_l0:
        links.arrive(m)
    outs = []
    for l in range(4):
        far = far0[l] + nt(l0[l], c0[4 * l]) + nt(l0[l + 1], c0[4 * l + 1])
        far = far + nt(l0[l + 5], c0[4 * l + 2]) + nt(l0[l + 6], c0[4 * l + 3])
        near[l] = near[l] + nt(far.astype(bf16), basis[l])
        copy = pltpu.make_async_copy(
            near.at[l], out_hbm.at[:, pl.ds(512 * l, 512)], out_sem.at[l]
        )
        copy.start()
        outs.append(copy)
    links.drain()
    for copy in outs:
        copy.wait()


def body(size, vectors, points, basis, near_list, e0, e1, e2, e3, c0, c1, c2, c3, c4):
    vecs, count = vectors.shape
    rank = basis.shape[1]
    anywhere = pl.BlockSpec(memory_space=pl.ANY)
    return pl.pallas_call(
        functools.partial(kernel, size),
        out_shape=jax.ShapeDtypeStruct((vecs, count), f32),
        in_specs=[anywhere] * 3
        + [pl.BlockSpec(memory_space=pltpu.SMEM)]
        + [anywhere] * 9,
        out_specs=anywhere,
        scratch_shapes=[
            pltpu.VMEM((4, 128, 512), f32),
            pltpu.VMEM((3, 2048), bf16),
            pltpu.VMEM((4, 512, 128), bf16),
            pltpu.VMEM((4, 128, 128), bf16),
            pltpu.VMEM((2, 128, 128), bf16),
            pltpu.VMEM((128, 128), bf16),
            pltpu.VMEM((128, 128), bf16),
            pltpu.VMEM((16, 128, 128), bf16),
            pltpu.VMEM((8, 128, 128), bf16),
            pltpu.VMEM((4, 128, 128), bf16),
            pltpu.VMEM((2, 128, 128), bf16),
            pltpu.VMEM((1, 128, 128), bf16),
            pltpu.VMEM((10, 128, 512), bf16),
            pltpu.VMEM((10, 128, 512), bf16),
            pltpu.VMEM((4, 512, 128), bf16),
            pltpu.VMEM((10, 128, 128), bf16),
            pltpu.VMEM((8, 128, 128), bf16),
            pltpu.VMEM((128, 128), bf16),
            pltpu.VMEM((4, 128, 128), bf16),
            pltpu.VMEM((128, 128), bf16),
            pltpu.VMEM((128, 128), bf16),
            pltpu.VMEM((128, 128), bf16),
            pltpu.VMEM((3, 128, 128), bf16),
            pltpu.VMEM((128, 128), bf16),
            pltpu.VMEM((2, 128, 128), bf16),
            pltpu.VMEM((128, 128), bf16),
            pltpu.VMEM((128, 128), bf16),
            pltpu.VMEM((128, 128), bf16),
            pltpu.VMEM((128, 128), bf16),
            pltpu.VMEM((128, 128), bf16),
            pltpu.VMEM((3, 128, 128), bf16),
            pltpu.VMEM((4, 128, 128), f32),
            pltpu.VMEM((4, 128, 512), f32),
            pltpu.SemaphoreType.DMA((24,)),
            pltpu.SemaphoreType.DMA((40,)),
            pltpu.SemaphoreType.DMA((40,)),
            pltpu.SemaphoreType.DMA((4,)),
        ],
        compiler_params=pltpu.CompilerParams(
            collective_id=0, has_side_effects=True, vmem_limit_bytes=48 * 2**20
        ),
        cost_estimate=pl.CostEstimate(
            flops=6_000_000_000, bytes_accessed=4_000_000, transcendentals=7_340_032
        ),
    )(
        vectors, points, basis, near_list,
        e0.reshape(-1, rank, rank), e1.reshape(-1, rank, rank), e2, e3,
        c0, c1, c2, c3, c4,
    )


def solution(mesh):
    placed = (
        P("vec", "leaf"),
        P(None, "leaf"),
        *[P("leaf", None)] * 6,
        *[P("leaf", None, None)] * 5,
    )
    return jax.shard_map(
        functools.partial(body, mesh.shape["leaf"]),
        mesh=mesh,
        in_specs=placed,
        out_specs=P("vec", "leaf"),
        check_vma=False,
    )
```

```python
import functools
import math

import jax
import jax.numpy as jnp
from jax import lax
from jax.experimental import pallas as pl
from jax.experimental.pallas import tpu as pltpu
from jax.sharding import PartitionSpec as P

MESH = pl.DeviceIdType.MESH
bf16 = jnp.bfloat16
f32 = jnp.float32
SCALE = 80.0 * math.log2(math.e)
NT = (((1,), (1,)), ((), ()))
offsets = (-3, -2, 2, 3)


def nn(a, b):
    return jnp.dot(a, b, preferred_element_type=f32)


def nt(a, b):
    return lax.dot_general(a, b, NT, preferred_element_type=f32)


def split3(value):
    high = value.astype(bf16).astype(f32)
    rest = value - high
    middle = rest.astype(bf16).astype(f32)
    low = (rest - middle).astype(bf16).astype(f32)
    return high, middle, low


def stack_rows(rows, count):
    width = rows[0].shape[1]
    place = lax.broadcasted_iota(jnp.int32, (count, width), 0)
    out = jnp.zeros((count, width), f32)
    for r, row in enumerate(rows):
        out = jnp.where(place == r, jnp.broadcast_to(row, (count, width)), out)
    return out


class Links:
    def __init__(self, send_sem, recv_sem, core):
        self.send_sem, self.recv_sem, self.core = send_sem, recv_sem, core
        self.sends = self.recvs = 0
        self.sent = []

    def copy(self, src, dst, target, send_slot, recv_slot):
        return pltpu.make_async_remote_copy(
            src_ref=src,
            dst_ref=dst,
            send_sem=self.send_sem.at[send_slot],
            recv_sem=self.recv_sem.at[recv_slot],
            device_id=(target, self.core),
            device_id_type=MESH,
        )

    def out(self, src, dst, target, recv_slot, valid=True):
        copy = self.copy(src, dst, target, self.sends, recv_slot)
        self.sends += 1
        self.sent.append((copy, valid))
        when(valid, copy.start)

    def drain(self):
        for copy, valid in self.sent:
            when(valid, copy.wait_send)


def when(valid, act):
    if valid is True:
        act()
    else:
        pl.when(valid)(act)


def kernel(
    size,
    vec_hbm, pts_hbm, basis_hbm, near_hbm, e0_hbm, e1_hbm, e2_hbm, e3_hbm,
    c0_hbm, c1_hbm, c2_hbm, c3_hbm, c4_hbm,
    out,
    vec_in, pts, basis, near_ref, e0, e1, e2, e3, c0, c1, c2, c3, c4,
    vw, gw, fw, ptd, ptf, x3, l0, l1, l2own, l2, p3s, p4s, l3r, l4r,
    f3s, f3r, f4s, f4r, far0,
    load_sem, send_sem, recv_sem,
):
    i = lax.axis_index("leaf")
    core = lax.axis_index("vec")
    half = i % 2
    y = i % 4
    two, four = i // 2, i // 4
    pair = i + 1 - 2 * half
    line = (pair, i + 2 - 4 * ((i // 2) % 2), i + 3 - 2 * y)

    def inside(d):
        return (d >= 0) & (d < size)

    three_to = (2 * (two + 3), 2 * (two + 2), 2 * (two - 2) + 1, 2 * (two - 3) + 1)
    three_from = [2 * (two - 3 + 5 * half + slot) + k for slot in range(2) for k in range(2)]
    four_to = [4 * (four - offsets[j]) + j for j in range(4)]
    my_offset = y - 3 + 3 * (y // 2)
    four_from = [4 * (four + my_offset) + k for k in range(4)]

    barrier = pltpu.get_barrier_semaphore()

    def greet(target):
        pl.semaphore_signal(barrier, inc=1, device_id=(target, core), device_id_type=MESH)

    wanted = jnp.int32(0)
    near_by = [i + move for move in (-3, -2, -1, 1, 2, 3)]
    for source in (*near_by, *three_from, *four_from):
        pl.when(inside(source))(functools.partial(greet, source))
    for target in (*near_by, *three_to, *four_to):
        wanted = wanted + inside(target).astype(jnp.int32)

    loads = []

    def load(src, dst):
        copy = pltpu.make_async_copy(src, dst, load_sem.at[len(loads)])
        copy.start()
        loads.append(copy)
        return copy

    load_vec = [
        load(vec_hbm.at[:, pl.ds(512 * l, 512)], vec_in.at[l]) for l in (3, 0, 2, 1)
    ]
    load_pts = load(pts_hbm, pts)
    e3_rows = e3.at[pl.ds(pl.multiple_of(64 * half, 64), 64)]
    load_e3 = load(e3_hbm, e3_rows)
    load_basis = [
        load(basis_hbm.at[pl.ds(512 * l, 512)], basis.at[l]) for l in range(4)
    ]
    load_e = [load(s, d) for s, d in ((e0_hbm, e0), (e1_hbm, e1), (e2_hbm, e2))]
    load_near = load(near_hbm, near_ref)
    load_c = [
        load(s, d)
        for s, d in ((c4_hbm, c4), (c3_hbm, c3), (c2_hbm, c2), (c1_hbm, c1), (c0_hbm, c0))
    ]

    def clear_all(*refs):
        for ref in refs:
            ref[...] = jnp.zeros(ref.shape, ref.dtype)

    pl.when(i < 1)(lambda: clear_all(vw.at[0:3], ptd.at[0:3], l0.at[0:3], l1.at[1:3]))
    pl.when(i < 2)(lambda: clear_all(l1.at[0:1], l2.at[1]))
    pl.when(i < 3)(lambda: clear_all(l2.at[0]))
    pl.when(i > size - 2)(lambda: clear_all(vw.at[7:10], ptd.at[7:10], l0.at[7:10], l1.at[5:7]))
    pl.when(i > size - 3)(lambda: clear_all(l1.at[7:8], l2.at[2]))
    pl.when(i > size - 4)(lambda: clear_all(l2.at[3]))
    for k in range(4):
        pl.when(jnp.logical_not(inside(three_from[k])))(functools.partial(clear_all, l3r.at[k]))
        pl.when(jnp.logical_not(inside(four_from[k])))(functools.partial(clear_all, l4r.at[k]))

    load_pts.wait()
    place = lax.broadcasted_iota(jnp.int32, (16, 128), 0)
    for l in range(4):
        x = pts[:, 512 * l : 512 * (l + 1)].astype(f32)
        dense = jnp.zeros((16, 128), f32)
        for k in range(3):
            for b in range(4):
                piece = jnp.broadcast_to(x[k : k + 1, 128 * b : 128 * (b + 1)], (16, 128))
                dense = jnp.where(place == 4 * k + b, piece, dense)
        ptd[3 + l] = dense.astype(bf16)
    for copy, l in zip(load_vec, (3, 0, 2, 1), strict=True):
        copy.wait()
        vw[3 + l] = vec_in[l].astype(bf16)
    load_e3.wait()

    links = Links(send_sem, recv_sem, core)
    slots = iter(range(40))
    arrivals = {}

    def arrival(name, dst, valid=True):
        slot = next(slots)
        arrivals[name] = (links.copy(dst, dst, pair, 0, slot), valid)
        return slot

    def arrive(*names):
        for name in names:
            copy, valid = arrivals[name]
            when(valid, copy.wait_recv)

    def shift(name, src, dst, move):
        slot = arrival(name, dst, inside(i - move))
        links.out(src, dst, i + move, slot, inside(i + move))

    def vec_out(k):
        shift(("vec", k, 0), vw.at[6 - k], vw.at[2 - k], 1)
        shift(("vec", k, 1), vw.at[3 + k], vw.at[7 + k], -1)

    pl.semaphore_wait(barrier, wanted)

    other_rows = e3.at[pl.ds(pl.multiple_of(64 - 64 * half, 64), 64)]
    slot = arrival("e3", other_rows)
    links.out(e3_rows, e3_rows, pair, slot)
    shift(("pts", 0), ptd.at[pl.ds(4, 3)], ptd.at[pl.ds(0, 3)], 1)
    shift(("pts", 1), ptd.at[pl.ds(3, 3)], ptd.at[pl.ds(7, 3)], -1)
    vec_out(0)

    for l in range(4):
        load_basis[l].wait()
        l0[3 + l] = nn(vw[3 + l], basis[l]).astype(bf16)
    load_e[0].wait()
    for t in range(2):
        l1[3 + t] = (nn(l0[3 + 2 * t], e0[2 * t]) + nn(l0[4 + 2 * t], e0[2 * t + 1])).astype(bf16)
    load_e[1].wait()
    l2own[...] = (nn(l1[3], e1[0]) + nn(l1[4], e1[1])).astype(bf16)
    load_e[2].wait()
    p3s[...] = nn(l2own[...], e2[...]).astype(bf16)

    slot3 = [arrival(("p3", k), l3r.at[k], inside(three_from[k])) for k in range(4)]
    for j, target in enumerate(three_to):
        row = 2 * (j % 2) + half
        links.out(p3s, l3r.at[row], target, slot3[0] + row, inside(target))
    shift(("l2", 0), l2own, l2.at[0], 3)
    shift(("l2", 1), l2own, l2.at[1], 2)
    shift(("l2", 2), l2own, l2.at[2], -2)
    shift(("l2", 3), l2own, l2.at[3], -3)
    shift(("l1", 0), l1.at[pl.ds(3, 2)], l1.at[pl.ds(1, 2)], 1)
    shift(("l1", 1), l1.at[pl.ds(3, 2)], l1.at[pl.ds(5, 2)], -1)
    shift(("l1", 2), l1.at[4], l1.at[0], 2)
    shift(("l1", 3), l1.at[3], l1.at[7], -2)
    vec_out(1)

    def source_factors(w):
        rows = [x3[w, pl.ds(k, 1), :] for k in range(3)]
        square = rows[0] * rows[0] + rows[1] * rows[1] + rows[2] * rows[2]
        squares = list(split3(square * (-0.5 * SCALE)))
        one = jnp.ones_like(square)
        scaled = [split3(row * SCALE) for row in rows]
        cols = [scaled[k][part] for part in range(3) for k in range(3)]
        gw[w, 0:16, :] = stack_rows(cols + [one] * 3 + squares, 16).astype(bf16)
        return rows, squares, one

    def spread(w):
        ptf[w] = ptd[w].astype(f32)
        for k in range(3):
            for b in range(4):
                x3[w, pl.ds(k, 1), 128 * b : 128 * (b + 1)] = ptf[w, pl.ds(4 * k + b, 1), :]

    gw[:, 16:, :] = jnp.zeros((10, 112, 512), bf16)
    for l in range(4):
        spread(3 + l)
        rows, squares, one = source_factors(3 + l)
        target_rows = stack_rows(rows * 3 + squares + [one] * 3, 16)
        padded = jnp.concatenate([target_rows, jnp.zeros((112, 512), f32)], axis=0)
        fw[l] = jnp.transpose(padded).astype(bf16)

    arrive("e3")
    p4s[...] = nn(p3s[...], e3[...]).astype(bf16)
    slot4 = [arrival(("p4", k), l4r.at[k], inside(four_from[k])) for k in range(4)]
    for target in four_to:
        links.out(p4s, l4r.at[y], target, slot4[0] + y, inside(target))
    vec_out(2)
    shift(("l0", 0), l0.at[pl.ds(4, 3)], l0.at[pl.ds(0, 3)], 1)
    shift(("l0", 1), l0.at[pl.ds(3, 3)], l0.at[pl.ds(7, 3)], -1)
    load_near.wait()

    def live(l, w):
        leaf = i * 4 + w - 3
        found = jnp.float32(0.0)
        for m in range(7):
            found = jnp.where(near_ref[l, m] == leaf, jnp.float32(1.0), found)
        return jnp.where(leaf >= 0, found, jnp.float32(0.0))

    def tile(l, w):
        block = jnp.exp2(nn(fw[l], gw[w])).astype(bf16)
        picked = vw[w] * live(l, w).astype(bf16)
        return nt(picked, block)

    def columns(l):
        return pl.ds(pl.multiple_of(512 * l, 512), 512)

    def own_leaf(l, carry):
        total = tile(l, 3)
        for w in range(4, 7):
            total = total + tile(l, w)
        out[:, columns(l)] = total
        return carry

    lax.fori_loop(0, 2, own_leaf, 0)

    for copy in load_c:
        copy.wait()
    arrive(*[("p3", k) for k in range(4)])
    far3 = jnp.zeros((128, 128), f32)
    for k in range(2):
        low3 = (l3r[2 * k].astype(f32) + l3r[2 * k + 1].astype(f32)).astype(bf16)
        far3 = far3 + nt(low3, c3[k])
    f3s[...] = far3.astype(bf16)
    links.out(f3s, f3r, pair, arrival("f3", f3r))
    arrive(*[("p4", k) for k in range(4)])
    low4 = l4r[0].astype(f32)
    for k in range(1, 4):
        low4 = low4 + l4r[k].astype(f32)
    far4 = nt(low4.astype(bf16), c4[0])
    f4s[...] = far4.astype(bf16)
    for k in range(3):
        links.out(f4s, f4r.at[k], line[k], arrival(("f4", k), f4r.at[k]))

    lax.fori_loop(2, 4, own_leaf, 0)

    arrive(("pts", 0), ("pts", 1))
    for w in (2, 7, 1, 8, 0, 9):
        spread(w)
        source_factors(w)

    def add(l, value):
        out[:, columns(l)] = out[:, columns(l)] + value

    def beside(l, carry):
        add(l, tile(l, 2))
        add(l + 1, tile(l + 1, 7))
        return carry

    arrive(("vec", 0, 0), ("vec", 0, 1))
    lax.fori_loop(0, 3, beside, 0)

    arrive(*[("l2", k) for k in range(4)], *[("l1", k) for k in range(4)])
    far2 = nt(l2[0], c2[0]) + nt(l2[1], c2[1]) + nt(l2[2], c2[2]) + nt(l2[3], c2[3])
    far1 = []
    for t in range(2):
        part = nt(l1[t], c1[4 * t]) + nt(l1[1 + t], c1[4 * t + 1])
        far1.append(part + nt(l1[5 + t], c1[4 * t + 2]) + nt(l1[6 + t], c1[4 * t + 3]))
    arrive("f3", *[("f4", k) for k in range(3)])
    down4 = far4
    for k in range(3):
        down4 = down4 + f4r[k].astype(f32)
    down3 = far3 + f3r[...].astype(f32) + nt(down4.astype(bf16), e3[...])
    down2 = (far2 + nt(down3.astype(bf16), e2[...])).astype(bf16)
    down1 = [(far1[t] + nt(down2, e1[t])).astype(bf16) for t in range(2)]
    for l in range(4):
        far0[l] = nt(down1[l // 2], e0[l])

    def second(l, carry):
        add(l, tile(l, 1))
        add(l + 2, tile(l + 2, 8))
        return carry

    arrive(("vec", 1, 0), ("vec", 1, 1))
    lax.fori_loop(0, 2, second, 0)
    arrive(("vec", 2, 0), ("vec", 2, 1))
    add(0, tile(0, 0))
    add(3, tile(3, 9))

    arrive(("l0", 0), ("l0", 1))
    for l in range(4):
        far = far0[l] + nt(l0[l], c0[4 * l]) + nt(l0[l + 1], c0[4 * l + 1])
        far = far + nt(l0[l + 5], c0[4 * l + 2]) + nt(l0[l + 6], c0[4 * l + 3])
        add(l, nt(far.astype(bf16), basis[l]))
    links.drain()


def body(size, vectors, points, basis, near_list, e0, e1, e2, e3, c0, c1, c2, c3, c4):
    vecs, count = vectors.shape
    rank = basis.shape[1]
    hbm = pl.BlockSpec(memory_space=pltpu.HBM)
    square = pltpu.VMEM((rank, rank), bf16)

    def squares(count):
        return pltpu.VMEM((count, rank, rank), bf16)

    return pl.pallas_call(
        functools.partial(kernel, size),
        out_shape=jax.ShapeDtypeStruct((vecs, count), f32),
        in_specs=[hbm] * 13,
        out_specs=pl.BlockSpec(memory_space=pltpu.VMEM),
        scratch_shapes=[
            pltpu.VMEM((4, 128, 512), f32),
            pltpu.VMEM((3, 2048), bf16),
            pltpu.VMEM((4, 512, 128), bf16),
            pltpu.SMEM((4, 7), jnp.int32),
            squares(4),
            squares(2),
            square,
            square,
            squares(16),
            squares(8),
            squares(4),
            squares(2),
            squares(1),
            pltpu.VMEM((10, 128, 512), bf16),
            pltpu.VMEM((10, 128, 512), bf16),
            pltpu.VMEM((4, 512, 128), bf16),
            pltpu.VMEM((10, 16, 128), bf16),
            pltpu.VMEM((10, 16, 128), f32),
            pltpu.VMEM((10, 8, 512), f32),
            squares(10),
            squares(8),
            square,
            squares(4),
            square,
            square,
            squares(4),
            squares(4),
            square,
            square,
            square,
            squares(3),
            pltpu.VMEM((4, 128, 128), f32),
            pltpu.SemaphoreType.DMA((24,)),
            pltpu.SemaphoreType.DMA((40,)),
            pltpu.SemaphoreType.DMA((40,)),
        ],
        compiler_params=pltpu.CompilerParams(
            collective_id=0, has_side_effects=True, vmem_limit_bytes=60 * 2**20
        ),
        cost_estimate=pl.CostEstimate(
            flops=6_000_000_000, bytes_accessed=4_000_000, transcendentals=7_340_032
        ),
    )(
        vectors, points, basis, near_list,
        e0.reshape(-1, rank, rank), e1.reshape(-1, rank, rank), e2, e3,
        c0, c1, c2, c3, c4,
    )


def solution(mesh):
    placed = (
        P("vec", "leaf"),
        P(None, "leaf"),
        *[P("leaf", None)] * 6,
        *[P("leaf", None, None)] * 5,
    )
    return jax.shard_map(
        functools.partial(body, mesh.shape["leaf"]),
        mesh=mesh,
        in_specs=placed,
        out_specs=P("vec", "leaf"),
        check_vma=False,
    )
```

```python
import functools
import math

import jax
import jax.numpy as jnp
from jax import lax
from jax.experimental import pallas as pl
from jax.experimental.pallas import tpu as pltpu
from jax.sharding import PartitionSpec as P

MESH = pl.DeviceIdType.MESH
bf16 = jnp.bfloat16
f32 = jnp.float32
SCALE = 80.0 * math.log2(math.e)
NT = (((1,), (1,)), ((), ()))
offsets = (-3, -2, 2, 3)
COPIES = 8


def nn(a, b):
    return jnp.dot(a, b, preferred_element_type=f32)


def nt(a, b):
    return lax.dot_general(a, b, NT, preferred_element_type=f32)


def split3(value):
    high = value.astype(bf16).astype(f32)
    rest = value - high
    middle = rest.astype(bf16).astype(f32)
    low = (rest - middle).astype(bf16).astype(f32)
    return high, middle, low


def stack_rows(rows, count):
    width = rows[0].shape[1]
    place = lax.broadcasted_iota(jnp.int32, (count, width), 0)
    out = jnp.zeros((count, width), f32)
    for r, row in enumerate(rows):
        out = jnp.where(place == r, jnp.broadcast_to(row, (count, width)), out)
    return out


class Links:
    def __init__(self, send_sem, recv_sem, core):
        self.send_sem, self.recv_sem, self.core = send_sem, recv_sem, core
        self.sends = self.recvs = 0
        self.sent = []

    def copy(self, src, dst, target, send_slot, recv_slot):
        return pltpu.make_async_remote_copy(
            src_ref=src,
            dst_ref=dst,
            send_sem=self.send_sem.at[send_slot],
            recv_sem=self.recv_sem.at[recv_slot],
            device_id=(target, self.core),
            device_id_type=MESH,
        )

    def out(self, src, dst, target, recv_slot, valid=True):
        copy = self.copy(src, dst, target, self.sends, recv_slot)
        self.sends += 1
        self.sent.append((copy, valid))
        when(valid, copy.start)

    def drain(self):
        for copy, valid in self.sent:
            when(valid, copy.wait_send)


def when(valid, act):
    if valid is True:
        act()
    else:
        pl.when(valid)(act)


def kernel(
    size,
    vec_hbm, pts_hbm, basis_hbm, near_hbm, e0_hbm, e1_hbm, e2_hbm, e3_hbm,
    c0_hbm, c1_hbm, c2_hbm, c3_hbm, c4_hbm,
    out,
    vec_in, pts, basis, near_ref, e0, e1, e2, e3, c0, c1, c2, c3, c4,
    vw, gw, fw, ptd, ptf, x3, l0, l1, l2own, l2, p3s, p4s, l3r, l4r,
    f3s, f3r, f4s, f4r, far0,
    load_sem, send_sem, recv_sem,
):
    i = lax.axis_index("leaf")
    core = lax.axis_index("vec")
    half = i % 2
    y = i % 4
    two, four = i // 2, i // 4
    pair = i + 1 - 2 * half
    line = (pair, i + 2 - 4 * ((i // 2) % 2), i + 3 - 2 * y)

    def inside(d):
        return (d >= 0) & (d < size)

    three_to = (2 * (two + 3), 2 * (two + 2), 2 * (two - 2) + 1, 2 * (two - 3) + 1)
    three_from = [2 * (two - 3 + 5 * half + slot) + k for slot in range(2) for k in range(2)]
    four_to = [4 * (four - offsets[j]) + j for j in range(4)]
    my_offset = y - 3 + 3 * (y // 2)
    four_from = [4 * (four + my_offset) + k for k in range(4)]

    barrier = pltpu.get_barrier_semaphore()

    def greet(target):
        pl.semaphore_signal(barrier, inc=1, device_id=(target, core), device_id_type=MESH)

    wanted = jnp.int32(0)
    near_by = [i + move for move in (-3, -2, -1, 1, 2, 3)]
    for source in (*near_by, *three_from, *four_from):
        pl.when(inside(source))(functools.partial(greet, source))
    for target in (*near_by, *three_to, *four_to):
        wanted = wanted + inside(target).astype(jnp.int32)

    loads = []

    def load(src, dst):
        copy = pltpu.make_async_copy(src, dst, load_sem.at[len(loads)])
        copy.start()
        loads.append(copy)
        return copy

    load_vec = [
        load(vec_hbm.at[:, pl.ds(512 * l, 512)], vec_in.at[l]) for l in (3, 0, 2, 1)
    ]
    load_pts = load(pts_hbm, pts)
    e3_rows = e3.at[pl.ds(pl.multiple_of(64 * half, 64), 64)]
    load_e3 = load(e3_hbm, e3_rows)
    load_basis = [
        load(basis_hbm.at[pl.ds(512 * l, 512)], basis.at[l]) for l in range(4)
    ]
    load_e = [load(s, d) for s, d in ((e0_hbm, e0), (e1_hbm, e1), (e2_hbm, e2))]
    load_near = load(near_hbm, near_ref)
    load_c = [
        load(s, d)
        for s, d in ((c4_hbm, c4), (c3_hbm, c3), (c2_hbm, c2), (c1_hbm, c1), (c0_hbm, c0))
    ]

    def clear_all(*refs):
        for ref in refs:
            ref[...] = jnp.zeros(ref.shape, ref.dtype)

    pl.when(i < 1)(lambda: clear_all(vw.at[0:3], ptd.at[0:3], l0.at[0:3], l1.at[1:3]))
    pl.when(i < 2)(lambda: clear_all(l1.at[0:1], l2.at[1]))
    pl.when(i < 3)(lambda: clear_all(l2.at[0]))
    pl.when(i > size - 2)(lambda: clear_all(vw.at[7:10], ptd.at[7:10], l0.at[7:10], l1.at[5:7]))
    pl.when(i > size - 3)(lambda: clear_all(l1.at[7:8], l2.at[2]))
    pl.when(i > size - 4)(lambda: clear_all(l2.at[3]))
    for k in range(4):
        pl.when(jnp.logical_not(inside(three_from[k])))(functools.partial(clear_all, l3r.at[k]))
        pl.when(jnp.logical_not(inside(four_from[k])))(functools.partial(clear_all, l4r.at[k]))

    load_pts.wait()
    place = lax.broadcasted_iota(jnp.int32, (16, 128), 0)
    for l in range(4):
        x = pts[:, 512 * l : 512 * (l + 1)].astype(f32)
        dense = jnp.zeros((16, 128), f32)
        for k in range(3):
            for b in range(4):
                piece = jnp.broadcast_to(x[k : k + 1, 128 * b : 128 * (b + 1)], (16, 128))
                dense = jnp.where(place == 4 * k + b, piece, dense)
        ptd[3 + l] = dense.astype(bf16)
    for copy, l in zip(load_vec, (3, 0, 2, 1), strict=True):
        copy.wait()
        vw[3 + l] = vec_in[l].astype(bf16)
    load_e3.wait()

    links = Links(send_sem, recv_sem, core)
    slots = iter(range(40))
    arrivals = {}

    def arrival(name, dst, valid=True):
        slot = next(slots)
        arrivals[name] = (links.copy(dst, dst, pair, 0, slot), valid)
        return slot

    def arrive(*names):
        for name in names:
            copy, valid = arrivals[name]
            when(valid, copy.wait_recv)

    def shift(name, src, dst, move):
        slot = arrival(name, dst, inside(i - move))
        links.out(src, dst, i + move, slot, inside(i + move))

    def vec_out(k):
        shift(("vec", k, 0), vw.at[6 - k], vw.at[2 - k], 1)
        shift(("vec", k, 1), vw.at[3 + k], vw.at[7 + k], -1)

    pl.semaphore_wait(barrier, wanted)

    other_rows = e3.at[pl.ds(pl.multiple_of(64 - 64 * half, 64), 64)]
    slot = arrival("e3", other_rows)
    links.out(e3_rows, e3_rows, pair, slot)
    shift(("pts", 0), ptd.at[pl.ds(4, 3)], ptd.at[pl.ds(0, 3)], 1)
    shift(("pts", 1), ptd.at[pl.ds(3, 3)], ptd.at[pl.ds(7, 3)], -1)
    vec_out(0)

    for l in range(4):
        load_basis[l].wait()
        l0[3 + l] = nn(vw[3 + l], basis[l]).astype(bf16)
    load_e[0].wait()
    for t in range(2):
        l1[3 + t] = (nn(l0[3 + 2 * t], e0[2 * t]) + nn(l0[4 + 2 * t], e0[2 * t + 1])).astype(bf16)
    load_e[1].wait()
    l2own[...] = (nn(l1[3], e1[0]) + nn(l1[4], e1[1])).astype(bf16)
    load_e[2].wait()
    p3s[...] = nn(l2own[...], e2[...]).astype(bf16)

    slot3 = [arrival(("p3", k), l3r.at[k], inside(three_from[k])) for k in range(4)]
    for j, target in enumerate(three_to):
        row = 2 * (j % 2) + half
        links.out(p3s, l3r.at[row], target, slot3[0] + row, inside(target))
    shift(("l2", 0), l2own, l2.at[0], 3)
    shift(("l2", 1), l2own, l2.at[1], 2)
    shift(("l2", 2), l2own, l2.at[2], -2)
    shift(("l2", 3), l2own, l2.at[3], -3)
    shift(("l1", 0), l1.at[pl.ds(3, 2)], l1.at[pl.ds(1, 2)], 1)
    shift(("l1", 1), l1.at[pl.ds(3, 2)], l1.at[pl.ds(5, 2)], -1)
    shift(("l1", 2), l1.at[4], l1.at[0], 2)
    shift(("l1", 3), l1.at[3], l1.at[7], -2)

    def source_factors(w):
        rows = [x3[w, pl.ds(k, 1), :] for k in range(3)]
        square = rows[0] * rows[0] + rows[1] * rows[1] + rows[2] * rows[2]
        squares = list(split3(square * (-0.5 * SCALE)))
        one = jnp.ones_like(square)
        scaled = [split3(row * SCALE) for row in rows]
        cols = [scaled[k][part] for part in range(3) for k in range(3)]
        gw[w, 0:16, :] = stack_rows(cols + [one] * 3 + squares, 16).astype(bf16)
        return rows, squares, one

    def spread(w):
        ptf[w] = ptd[w].astype(f32)
        for k in range(3):
            for b in range(4):
                x3[w, pl.ds(k, 1), 128 * b : 128 * (b + 1)] = ptf[w, pl.ds(4 * k + b, 1), :]

    gw[:, 16:, :] = jnp.zeros((10, 112, 512), bf16)
    for l in range(4):
        spread(3 + l)
        rows, squares, one = source_factors(3 + l)
        target_rows = stack_rows(rows * 3 + squares + [one] * 3, 16)
        padded = jnp.concatenate([target_rows, jnp.zeros((112, 512), f32)], axis=0)
        fw[l] = jnp.transpose(padded).astype(bf16)

    arrive("e3")
    p4s[...] = nn(p3s[...], e3[...]).astype(bf16)
    slot4 = [arrival(("p4", k), l4r.at[k], inside(four_from[k])) for k in range(4)]
    for target in four_to:
        links.out(p4s, l4r.at[y], target, slot4[0] + y, inside(target))
    load_near.wait()

    def live(l, w):
        leaf = i * 4 + w - 3
        found = jnp.float32(0.0)
        for m in range(7):
            found = jnp.where(near_ref[l, m] == leaf, jnp.float32(1.0), found)
        return jnp.where(leaf >= 0, found, jnp.float32(0.0))

    def tile(l, w):
        block = jnp.exp2(nn(fw[l], gw[w])).astype(bf16)
        picked = vw[w] * live(l, w).astype(bf16)
        return nt(picked, block)

    def columns(l):
        return pl.ds(pl.multiple_of(512 * l, 512), 512)

    def own_leaf(l, carry):
        total = tile(l, 3)
        for w in range(4, 7):
            total = total + tile(l, w)
        out[:, columns(l)] = total
        return carry

    def add(l, value):
        out[:, columns(l)] = out[:, columns(l)] + value

    lax.fori_loop(0, 1, own_leaf, 0)
    vec_out(1)
    lax.fori_loop(1, 2, own_leaf, 0)

    lax.fori_loop(2, 3, own_leaf, 0)
    shift(("l0", 0), l0.at[pl.ds(4, 3)], l0.at[pl.ds(0, 3)], 1)
    shift(("l0", 1), l0.at[pl.ds(3, 3)], l0.at[pl.ds(7, 3)], -1)

    for copy in load_c:
        copy.wait()
    arrive(*[("p3", k) for k in range(4)])
    far3 = jnp.zeros((128, 128), f32)
    for k in range(2):
        low3 = (l3r[2 * k].astype(f32) + l3r[2 * k + 1].astype(f32)).astype(bf16)
        far3 = far3 + nt(low3, c3[k])
    f3s[...] = far3.astype(bf16)
    links.out(f3s, f3r, pair, arrival("f3", f3r))
    arrive(*[("p4", k) for k in range(4)])
    low4 = l4r[0].astype(f32)
    for k in range(1, 4):
        low4 = low4 + l4r[k].astype(f32)
    far4 = nt(low4.astype(bf16), c4[0])
    f4s[...] = far4.astype(bf16)
    for k in range(3):
        links.out(f4s, f4r.at[k], line[k], arrival(("f4", k), f4r.at[k]))
    vec_out(2)

    lax.fori_loop(3, 4, own_leaf, 0)

    arrive(("pts", 0), ("pts", 1))
    for w in (2, 7, 1, 8, 0, 9):
        spread(w)
        source_factors(w)

    def beside(l, carry):
        add(l, tile(l, 2))
        add(l + 1, tile(l + 1, 7))
        return carry

    arrive(("vec", 0, 0), ("vec", 0, 1))
    lax.fori_loop(0, 3, beside, 0)

    def second(l, carry):
        add(l, tile(l, 1))
        add(l + 2, tile(l + 2, 8))
        return carry

    arrive(("vec", 1, 0), ("vec", 1, 1))
    lax.fori_loop(0, 2, second, 0)

    arrive(*[("l2", k) for k in range(4)], *[("l1", k) for k in range(4)])
    far2 = nt(l2[0], c2[0]) + nt(l2[1], c2[1]) + nt(l2[2], c2[2]) + nt(l2[3], c2[3])
    far1 = []
    for t in range(2):
        part = nt(l1[t], c1[4 * t]) + nt(l1[1 + t], c1[4 * t + 1])
        far1.append(part + nt(l1[5 + t], c1[4 * t + 2]) + nt(l1[6 + t], c1[4 * t + 3]))
    arrive(("l0", 0), ("l0", 1))
    for l in range(4):
        far = nt(l0[l], c0[4 * l]) + nt(l0[l + 1], c0[4 * l + 1])
        far0[l] = far + nt(l0[l + 5], c0[4 * l + 2]) + nt(l0[l + 6], c0[4 * l + 3])
    arrive("f3", *[("f4", k) for k in range(3)])
    down4 = far4
    for k in range(3):
        down4 = down4 + f4r[k].astype(f32)
    down3 = far3 + f3r[...].astype(f32) + nt(down4.astype(bf16), e3[...])
    down2 = (far2 + nt(down3.astype(bf16), e2[...])).astype(bf16)
    down1 = [(far1[t] + nt(down2, e1[t])).astype(bf16) for t in range(2)]
    for l in range(4):
        down0 = (far0[l] + nt(down1[l // 2], e0[l])).astype(bf16)
        add(l, nt(down0, basis[l]))

    arrive(("vec", 2, 0), ("vec", 2, 1))
    add(0, tile(0, 0))
    add(3, tile(3, 9))
    links.drain()


def hand_on(source, target, sem):
    rows = source.shape[0] // COPIES
    parts = [pl.ds(rows * k, rows) for k in range(COPIES)]
    copies = [
        pltpu.make_async_copy(source.at[part], target.at[part], sem.at[k])
        for k, part in enumerate(parts)
    ]
    for copy in copies:
        copy.start()
    for copy in copies:
        copy.wait()


def body(size, vectors, points, basis, near_list, e0, e1, e2, e3, c0, c1, c2, c3, c4):
    vecs, count = vectors.shape
    rank = basis.shape[1]
    hbm = pl.BlockSpec(memory_space=pltpu.HBM)
    square = pltpu.VMEM((rank, rank), bf16)

    def squares(count):
        return pltpu.VMEM((count, rank, rank), bf16)

    operands = (
        vectors, points, basis, near_list,
        e0.reshape(-1, rank, rank), e1.reshape(-1, rank, rank), e2, e3,
        c0, c1, c2, c3, c4,
    )
    result = pl.pallas_call(
        functools.partial(kernel, size),
        out_shape=pltpu.VMEM((vecs, count), f32),
        in_specs=[hbm] * 13,
        out_specs=pl.BlockSpec(memory_space=pltpu.VMEM),
        scratch_shapes=[
            pltpu.VMEM((4, 128, 512), f32),
            pltpu.VMEM((3, 2048), bf16),
            pltpu.VMEM((4, 512, 128), bf16),
            pltpu.SMEM((4, 7), jnp.int32),
            squares(4),
            squares(2),
            square,
            square,
            squares(16),
            squares(8),
            squares(4),
            squares(2),
            squares(1),
            pltpu.VMEM((10, 128, 512), bf16),
            pltpu.VMEM((10, 128, 512), bf16),
            pltpu.VMEM((4, 512, 128), bf16),
            pltpu.VMEM((10, 16, 128), bf16),
            pltpu.VMEM((10, 16, 128), f32),
            pltpu.VMEM((10, 8, 512), f32),
            squares(10),
            squares(8),
            square,
            squares(4),
            square,
            square,
            squares(4),
            squares(4),
            square,
            square,
            square,
            squares(3),
            pltpu.VMEM((4, 128, 128), f32),
            pltpu.SemaphoreType.DMA((24,)),
            pltpu.SemaphoreType.DMA((40,)),
            pltpu.SemaphoreType.DMA((40,)),
        ],
        compiler_params=pltpu.CompilerParams(
            collective_id=0, has_side_effects=True, vmem_limit_bytes=40 * 2**20
        ),
        cost_estimate=pl.CostEstimate(
            flops=6_000_000_000, bytes_accessed=4_000_000, transcendentals=7_340_032
        ),
    )(*[pltpu.with_memory_space_constraint(x, pltpu.HBM) for x in operands])
    return pl.pallas_call(
        hand_on,
        out_shape=jax.ShapeDtypeStruct((vecs, count), f32),
        in_specs=[pl.BlockSpec(memory_space=pltpu.VMEM)],
        out_specs=hbm,
        scratch_shapes=[
            pltpu.SemaphoreType.DMA((COPIES,)),
        ],
        compiler_params=pltpu.CompilerParams(vmem_limit_bytes=16 * 2**20),
    )(result)


def solution(mesh):
    placed = (
        P("vec", "leaf"),
        P(None, "leaf"),
        *[P("leaf", None)] * 6,
        *[P("leaf", None, None)] * 5,
    )
    return jax.shard_map(
        functools.partial(body, mesh.shape["leaf"]),
        mesh=mesh,
        in_specs=placed,
        out_specs=P("vec", "leaf"),
        check_vma=False,
    )
```

```python
import functools
import math

import jax
import jax.numpy as jnp
from jax import lax
from jax.experimental import pallas as pl
from jax.experimental.pallas import tpu as pltpu
from jax.sharding import PartitionSpec as P

MESH = pl.DeviceIdType.MESH
bf16 = jnp.bfloat16
f32 = jnp.float32
SCALE = 80.0 * math.log2(math.e)
NT = (((1,), (1,)), ((), ()))
offsets = (-3, -2, 2, 3)
COPIES = 8


def nn(a, b):
    return jnp.dot(a, b, preferred_element_type=f32)


def nt(a, b):
    return lax.dot_general(a, b, NT, preferred_element_type=f32)


def split3(value):
    high = value.astype(bf16).astype(f32)
    rest = value - high
    middle = rest.astype(bf16).astype(f32)
    low = (rest - middle).astype(bf16).astype(f32)
    return high, middle, low


def stack_rows(rows, count):
    width = rows[0].shape[1]
    place = lax.broadcasted_iota(jnp.int32, (count, width), 0)
    out = jnp.zeros((count, width), f32)
    for r, row in enumerate(rows):
        out = jnp.where(place == r, jnp.broadcast_to(row, (count, width)), out)
    return out


class Links:
    def __init__(self, send_sem, recv_sem, core):
        self.send_sem, self.recv_sem, self.core = send_sem, recv_sem, core
        self.sends = self.recvs = 0
        self.sent = []

    def copy(self, src, dst, target, send_slot, recv_slot):
        return pltpu.make_async_remote_copy(
            src_ref=src,
            dst_ref=dst,
            send_sem=self.send_sem.at[send_slot],
            recv_sem=self.recv_sem.at[recv_slot],
            device_id=(target, self.core),
            device_id_type=MESH,
        )

    def out(self, src, dst, target, recv_slot, valid=True):
        copy = self.copy(src, dst, target, self.sends, recv_slot)
        self.sends += 1
        self.sent.append((copy, valid))
        when(valid, copy.start)

    def drain(self):
        for copy, valid in self.sent:
            when(valid, copy.wait_send)


def when(valid, act):
    if valid is True:
        act()
    else:
        pl.when(valid)(act)


def kernel(
    size,
    vec_hbm, pts_hbm, basis_hbm, near_hbm, e0_hbm, e1_hbm, e2_hbm, e3_hbm,
    c0_hbm, c1_hbm, c2_hbm, c3_hbm, c4_hbm,
    out,
    vec_in, pts, basis, near_ref, e0, e1, e2, e3, c0, c1, c2, c3, c4,
    vw, gw, fw, ptd, ptf, x3, l0, l1, l2own, l2, p3s, p4s, l3r, l4r,
    f3s, f3r, f4s, f4r, far0,
    load_sem, send_sem, recv_sem,
):
    i = lax.axis_index("leaf")
    core = lax.axis_index("vec")
    half = i % 2
    y = i % 4
    two, four = i // 2, i // 4
    pair = i + 1 - 2 * half
    line = (pair, i + 2 - 4 * ((i // 2) % 2), i + 3 - 2 * y)

    def inside(d):
        return (d >= 0) & (d < size)

    three_to = (2 * (two + 3), 2 * (two + 2), 2 * (two - 2) + 1, 2 * (two - 3) + 1)
    three_from = [2 * (two - 3 + 5 * half + slot) + k for slot in range(2) for k in range(2)]
    four_to = [4 * (four - offsets[j]) + j for j in range(4)]
    my_offset = y - 3 + 3 * (y // 2)
    four_from = [4 * (four + my_offset) + k for k in range(4)]

    barrier = pltpu.get_barrier_semaphore()

    def greet(target):
        pl.semaphore_signal(barrier, inc=1, device_id=(target, core), device_id_type=MESH)

    wanted = jnp.int32(0)
    near_by = [i + move for move in (-3, -2, -1, 1, 2, 3)]
    for source in (*near_by, *three_from, *four_from):
        pl.when(inside(source))(functools.partial(greet, source))
    for target in (*near_by, *three_to, *four_to):
        wanted = wanted + inside(target).astype(jnp.int32)

    loads = []

    def load(src, dst):
        copy = pltpu.make_async_copy(src, dst, load_sem.at[len(loads)])
        copy.start()
        loads.append(copy)
        return copy

    def load_leaf(l):
        return load(vec_hbm.at[:, pl.ds(512 * l, 512)], vec_in.at[l])

    load_vec = {l: load_leaf(l) for l in (3, 0)}
    load_pts = load(pts_hbm, pts)
    e3_rows = e3.at[pl.ds(pl.multiple_of(64 * half, 64), 64)]
    load_e3 = load(e3_hbm, e3_rows)
    load_vec.update({l: load_leaf(l) for l in (2, 1)})
    load_basis = [
        load(basis_hbm.at[pl.ds(512 * l, 512)], basis.at[l]) for l in range(4)
    ]
    load_e = [load(s, d) for s, d in ((e0_hbm, e0), (e1_hbm, e1), (e2_hbm, e2))]
    load_near = load(near_hbm, near_ref)
    load_c = [
        load(s, d)
        for s, d in ((c4_hbm, c4), (c3_hbm, c3), (c2_hbm, c2), (c1_hbm, c1), (c0_hbm, c0))
    ]

    def clear_all(*refs):
        for ref in refs:
            ref[...] = jnp.zeros(ref.shape, ref.dtype)

    pl.when(i < 1)(lambda: clear_all(vw.at[0:3], ptd.at[0:3], l0.at[0:3], l1.at[1:3]))
    pl.when(i < 2)(lambda: clear_all(l1.at[0:1], l2.at[1]))
    pl.when(i < 3)(lambda: clear_all(l2.at[0]))
    pl.when(i > size - 2)(lambda: clear_all(vw.at[7:10], ptd.at[7:10], l0.at[7:10], l1.at[5:7]))
    pl.when(i > size - 3)(lambda: clear_all(l1.at[7:8], l2.at[2]))
    pl.when(i > size - 4)(lambda: clear_all(l2.at[3]))
    for k in range(4):
        pl.when(jnp.logical_not(inside(three_from[k])))(functools.partial(clear_all, l3r.at[k]))
        pl.when(jnp.logical_not(inside(four_from[k])))(functools.partial(clear_all, l4r.at[k]))

    def take_leaf(l):
        load_vec[l].wait()
        vw[3 + l] = vec_in[l].astype(bf16)

    take_leaf(3)
    take_leaf(0)
    load_e3.wait()

    links = Links(send_sem, recv_sem, core)
    slots = iter(range(40))
    arrivals = {}

    def arrival(name, dst, valid=True):
        slot = next(slots)
        arrivals[name] = (links.copy(dst, dst, pair, 0, slot), valid)
        return slot

    def arrive(*names):
        for name in names:
            copy, valid = arrivals[name]
            when(valid, copy.wait_recv)

    def shift(name, src, dst, move):
        slot = arrival(name, dst, inside(i - move))
        links.out(src, dst, i + move, slot, inside(i + move))

    def vec_out(k):
        shift(("vec", k, 0), vw.at[6 - k], vw.at[2 - k], 1)
        shift(("vec", k, 1), vw.at[3 + k], vw.at[7 + k], -1)

    pl.semaphore_wait(barrier, wanted)

    other_rows = e3.at[pl.ds(pl.multiple_of(64 - 64 * half, 64), 64)]
    slot = arrival("e3", other_rows)
    links.out(e3_rows, e3_rows, pair, slot)
    vec_out(0)
    take_leaf(2)
    take_leaf(1)

    for l in range(4):
        load_basis[l].wait()
        l0[3 + l] = nn(vw[3 + l], basis[l]).astype(bf16)
    load_e[0].wait()
    for t in range(2):
        l1[3 + t] = (nn(l0[3 + 2 * t], e0[2 * t]) + nn(l0[4 + 2 * t], e0[2 * t + 1])).astype(bf16)
    load_e[1].wait()
    l2own[...] = (nn(l1[3], e1[0]) + nn(l1[4], e1[1])).astype(bf16)
    load_e[2].wait()
    p3s[...] = nn(l2own[...], e2[...]).astype(bf16)

    slot3 = [arrival(("p3", k), l3r.at[k], inside(three_from[k])) for k in range(4)]
    for j, target in enumerate(three_to):
        row = 2 * (j % 2) + half
        links.out(p3s, l3r.at[row], target, slot3[0] + row, inside(target))
    shift(("l2", 0), l2own, l2.at[0], 3)
    shift(("l2", 1), l2own, l2.at[1], 2)
    shift(("l2", 2), l2own, l2.at[2], -2)
    shift(("l2", 3), l2own, l2.at[3], -3)
    shift(("l1", 0), l1.at[pl.ds(3, 2)], l1.at[pl.ds(1, 2)], 1)
    shift(("l1", 1), l1.at[pl.ds(3, 2)], l1.at[pl.ds(5, 2)], -1)
    shift(("l1", 2), l1.at[4], l1.at[0], 2)
    shift(("l1", 3), l1.at[3], l1.at[7], -2)

    load_pts.wait()
    place = lax.broadcasted_iota(jnp.int32, (16, 128), 0)
    for l in range(4):
        x = pts[:, 512 * l : 512 * (l + 1)].astype(f32)
        dense = jnp.zeros((16, 128), f32)
        for k in range(3):
            for b in range(4):
                piece = jnp.broadcast_to(x[k : k + 1, 128 * b : 128 * (b + 1)], (16, 128))
                dense = jnp.where(place == 4 * k + b, piece, dense)
        ptd[3 + l] = dense.astype(bf16)
    shift(("pts", 0), ptd.at[pl.ds(4, 3)], ptd.at[pl.ds(0, 3)], 1)
    shift(("pts", 1), ptd.at[pl.ds(3, 3)], ptd.at[pl.ds(7, 3)], -1)

    def source_factors(w):
        rows = [x3[w, pl.ds(k, 1), :] for k in range(3)]
        square = rows[0] * rows[0] + rows[1] * rows[1] + rows[2] * rows[2]
        squares = list(split3(square * (-0.5 * SCALE)))
        one = jnp.ones_like(square)
        scaled = [split3(row * SCALE) for row in rows]
        cols = [scaled[k][part] for part in range(3) for k in range(3)]
        gw[w, 0:16, :] = stack_rows(cols + [one] * 3 + squares, 16).astype(bf16)
        return rows, squares, one

    def spread(w):
        ptf[w] = ptd[w].astype(f32)
        for k in range(3):
            for b in range(4):
                x3[w, pl.ds(k, 1), 128 * b : 128 * (b + 1)] = ptf[w, pl.ds(4 * k + b, 1), :]

    gw[:, 16:, :] = jnp.zeros((10, 112, 512), bf16)
    for l in range(4):
        spread(3 + l)
        rows, squares, one = source_factors(3 + l)
        target_rows = stack_rows(rows * 3 + squares + [one] * 3, 16)
        padded = jnp.concatenate([target_rows, jnp.zeros((112, 512), f32)], axis=0)
        fw[l] = jnp.transpose(padded).astype(bf16)

    arrive("e3")
    p4s[...] = nn(p3s[...], e3[...]).astype(bf16)
    slot4 = [arrival(("p4", k), l4r.at[k], inside(four_from[k])) for k in range(4)]
    for target in four_to:
        links.out(p4s, l4r.at[y], target, slot4[0] + y, inside(target))
    load_near.wait()

    def live(l, w):
        leaf = i * 4 + w - 3
        found = jnp.float32(0.0)
        for m in range(7):
            found = jnp.where(near_ref[l, m] == leaf, jnp.float32(1.0), found)
        return jnp.where(leaf >= 0, found, jnp.float32(0.0))

    def tile(l, w):
        block = jnp.exp2(nn(fw[l], gw[w])).astype(bf16)
        picked = vw[w] * live(l, w).astype(bf16)
        return nt(picked, block)

    def columns(l):
        return pl.ds(pl.multiple_of(512 * l, 512), 512)

    def own_leaf(l, carry):
        total = tile(l, 3)
        for w in range(4, 7):
            total = total + tile(l, w)
        out[:, columns(l)] = total
        return carry

    def add(l, value):
        out[:, columns(l)] = out[:, columns(l)] + value

    lax.fori_loop(0, 1, own_leaf, 0)
    vec_out(1)
    lax.fori_loop(1, 2, own_leaf, 0)

    lax.fori_loop(2, 3, own_leaf, 0)
    shift(("l0", 0), l0.at[pl.ds(4, 3)], l0.at[pl.ds(0, 3)], 1)
    shift(("l0", 1), l0.at[pl.ds(3, 3)], l0.at[pl.ds(7, 3)], -1)

    for copy in load_c:
        copy.wait()
    arrive(*[("p3", k) for k in range(4)])
    far3 = jnp.zeros((128, 128), f32)
    for k in range(2):
        low3 = (l3r[2 * k].astype(f32) + l3r[2 * k + 1].astype(f32)).astype(bf16)
        far3 = far3 + nt(low3, c3[k])
    f3s[...] = far3.astype(bf16)
    links.out(f3s, f3r, pair, arrival("f3", f3r))
    arrive(*[("p4", k) for k in range(4)])
    low4 = l4r[0].astype(f32)
    for k in range(1, 4):
        low4 = low4 + l4r[k].astype(f32)
    far4 = nt(low4.astype(bf16), c4[0])
    f4s[...] = far4.astype(bf16)
    for k in range(3):
        links.out(f4s, f4r.at[k], line[k], arrival(("f4", k), f4r.at[k]))
    vec_out(2)

    lax.fori_loop(3, 4, own_leaf, 0)

    arrive(("pts", 0), ("pts", 1))
    for w in (2, 7, 1, 8, 0, 9):
        spread(w)
        source_factors(w)

    def beside(l, carry):
        add(l, tile(l, 2))
        add(l + 1, tile(l + 1, 7))
        return carry

    arrive(("vec", 0, 0), ("vec", 0, 1))
    lax.fori_loop(0, 3, beside, 0)

    def second(l, carry):
        add(l, tile(l, 1))
        add(l + 2, tile(l + 2, 8))
        return carry

    arrive(("vec", 1, 0), ("vec", 1, 1))
    lax.fori_loop(0, 2, second, 0)

    arrive(*[("l2", k) for k in range(4)], *[("l1", k) for k in range(4)])
    far2 = nt(l2[0], c2[0]) + nt(l2[1], c2[1]) + nt(l2[2], c2[2]) + nt(l2[3], c2[3])
    far1 = []
    for t in range(2):
        part = nt(l1[t], c1[4 * t]) + nt(l1[1 + t], c1[4 * t + 1])
        far1.append(part + nt(l1[5 + t], c1[4 * t + 2]) + nt(l1[6 + t], c1[4 * t + 3]))
    arrive(("l0", 0), ("l0", 1))
    for l in range(4):
        far = nt(l0[l], c0[4 * l]) + nt(l0[l + 1], c0[4 * l + 1])
        far0[l] = far + nt(l0[l + 5], c0[4 * l + 2]) + nt(l0[l + 6], c0[4 * l + 3])
    arrive("f3", *[("f4", k) for k in range(3)])
    down4 = far4
    for k in range(3):
        down4 = down4 + f4r[k].astype(f32)
    down3 = far3 + f3r[...].astype(f32) + nt(down4.astype(bf16), e3[...])
    down2 = (far2 + nt(down3.astype(bf16), e2[...])).astype(bf16)
    down1 = [(far1[t] + nt(down2, e1[t])).astype(bf16) for t in range(2)]
    for l in range(4):
        down0 = (far0[l] + nt(down1[l // 2], e0[l])).astype(bf16)
        add(l, nt(down0, basis[l]))

    arrive(("vec", 2, 0), ("vec", 2, 1))
    add(0, tile(0, 0))
    add(3, tile(3, 9))
    links.drain()


def hand_on(source, target, sem):
    rows = source.shape[0] // COPIES
    parts = [pl.ds(rows * k, rows) for k in range(COPIES)]
    copies = [
        pltpu.make_async_copy(source.at[part], target.at[part], sem.at[k])
        for k, part in enumerate(parts)
    ]
    for copy in copies:
        copy.start()
    for copy in copies:
        copy.wait()


def body(size, vectors, points, basis, near_list, e0, e1, e2, e3, c0, c1, c2, c3, c4):
    vecs, count = vectors.shape
    rank = basis.shape[1]
    hbm = pl.BlockSpec(memory_space=pltpu.HBM)
    square = pltpu.VMEM((rank, rank), bf16)

    def squares(count):
        return pltpu.VMEM((count, rank, rank), bf16)

    operands = (
        vectors, points, basis, near_list,
        e0.reshape(-1, rank, rank), e1.reshape(-1, rank, rank), e2, e3,
        c0, c1, c2, c3, c4,
    )
    result = pl.pallas_call(
        functools.partial(kernel, size),
        out_shape=pltpu.VMEM((vecs, count), f32),
        in_specs=[hbm] * 13,
        out_specs=pl.BlockSpec(memory_space=pltpu.VMEM),
        scratch_shapes=[
            pltpu.VMEM((4, 128, 512), f32),
            pltpu.VMEM((3, 2048), bf16),
            pltpu.VMEM((4, 512, 128), bf16),
            pltpu.SMEM((4, 7), jnp.int32),
            squares(4),
            squares(2),
            square,
            square,
            squares(16),
            squares(8),
            squares(4),
            squares(2),
            squares(1),
            pltpu.VMEM((10, 128, 512), bf16),
            pltpu.VMEM((10, 128, 512), bf16),
            pltpu.VMEM((4, 512, 128), bf16),
            pltpu.VMEM((10, 16, 128), bf16),
            pltpu.VMEM((10, 16, 128), f32),
            pltpu.VMEM((10, 8, 512), f32),
            squares(10),
            squares(8),
            square,
            squares(4),
            square,
            square,
            squares(4),
            squares(4),
            square,
            square,
            square,
            squares(3),
            pltpu.VMEM((4, 128, 128), f32),
            pltpu.SemaphoreType.DMA((24,)),
            pltpu.SemaphoreType.DMA((40,)),
            pltpu.SemaphoreType.DMA((40,)),
        ],
        compiler_params=pltpu.CompilerParams(
            collective_id=0, has_side_effects=True, vmem_limit_bytes=40 * 2**20
        ),
        cost_estimate=pl.CostEstimate(
            flops=6_000_000_000, bytes_accessed=4_000_000, transcendentals=7_340_032
        ),
    )(*[pltpu.with_memory_space_constraint(x, pltpu.HBM) for x in operands])
    return pl.pallas_call(
        hand_on,
        out_shape=jax.ShapeDtypeStruct((vecs, count), f32),
        in_specs=[pl.BlockSpec(memory_space=pltpu.VMEM)],
        out_specs=hbm,
        scratch_shapes=[
            pltpu.SemaphoreType.DMA((COPIES,)),
        ],
        compiler_params=pltpu.CompilerParams(vmem_limit_bytes=16 * 2**20),
    )(result)


def solution(mesh):
    placed = (
        P("vec", "leaf"),
        P(None, "leaf"),
        *[P("leaf", None)] * 6,
        *[P("leaf", None, None)] * 5,
    )
    return jax.shard_map(
        functools.partial(body, mesh.shape["leaf"]),
        mesh=mesh,
        in_specs=placed,
        out_specs=P("vec", "leaf"),
        check_vma=False,
    )
```
